32 devices in a mesh: dp: 4 (over y, x), mp: 8 (over z, core).
Axes of the slice: x: 2, y: 2, z: 4, core: 2. Of those that a mesh axis runs over, the one named last changes fastest.
Arguments:
- hidden: bfloat16 [32, 128, 18432], P('dp', None, 'mp'), may hold values from -400 to 400
- cotangent: bfloat16 [32, 128, 4608], P('dp', 'mp'), may hold values from -8 to 8
- w_down: bfloat16 [18432, 4608], P('mp', 'dp'), may hold values from -0.046875 to 0.046875
- lengths: int32 [32], P('dp'), may hold values from 1 to 128, 3072 in all
Outputs:
- weight_grad: float32 [18432, 4608], P('mp', 'dp')
- d_hidden: bfloat16 [32, 128, 18432], P('dp', None, 'mp')
The draws below stay inside these ranges and needn't reach their ends.
All inputs are finite; a program needn't handle non-finite values. No bound on the sum of `lengths` on one device may be relied on, other than what follows from the above.
Results may differ from the reference program's by a relative error of at most 0.003.
Values may be sent and summed in bfloat16 or wider, within the bound.
A program may use at most 448 MiB of HBM per device.

```python
import math
import jax
import jax.numpy as jnp
import numpy as np
from jax import lax

D = 4608
FF = 18432
SEQ = 128
BATCH = 32


def draw_hidden(key, part):
    key_base = jax.random.fold_in(key, 11)
    key_rows = jax.random.fold_in(key, 12)
    key_cols = jax.random.fold_in(key, 13)
    key_common = jax.random.fold_in(key, 14)
    rising = jnp.arange(FF, dtype=jnp.float32) / FF
    base = jax.random.truncated_normal(key_base, -4.0, 4.0, (BATCH, SEQ, FF), jnp.float32)
    col_power = 0.5 * rising + 0.5 * jax.random.uniform(key_cols, (FF,), jnp.float32)
    common = 2.0 * jax.random.truncated_normal(key_common, -4.0, 4.0, (BATCH, 1, FF), jnp.float32)
    row_power = jax.random.uniform(key_rows, (BATCH, SEQ, 1), jnp.float32)
    mixed = 0.8 * base * jnp.power(10.0, row_power) + common
    return (mixed * jnp.power(10.0, col_power)[None, None, :]).astype(jnp.bfloat16)


def draw_cotangent(key, part):
    key_base = jax.random.fold_in(key, 21)
    key_common = jax.random.fold_in(key, 22)
    base = jax.random.truncated_normal(key_base, -4.0, 4.0, (BATCH, SEQ, D), jnp.float32)
    common = jax.random.truncated_normal(key_common, -4.0, 4.0, (BATCH, 1, D), jnp.float32)
    return (base + common).astype(jnp.bfloat16)


def block_scale(key, extent, shards, smallest, largest):
    factor_of = 1.0
    for dim, blocks in shards:
        draws = jax.random.uniform(jax.random.fold_in(jax.random.fold_in(key, 6), dim), (blocks,), jnp.float32, smallest / len(shards), largest / len(shards))
        factor_of = factor_of * jnp.repeat(jnp.exp(draws), extent[dim] // blocks).reshape((-1,) + (1,) * (len(extent) - 1 - dim))
    return factor_of


def split_up(count, total, most, skew):
    weights = [(1 << 20) // math.isqrt(rank ** skew) + 1 for rank in range(2, count + 1)]
    spare, holding = total - most - (count - 1), [1] * (count - 1)
    while spare > 0:
        candidates = [i for i in range(count - 1) if holding[i] < most]
        whole, budget = sum([weights[i] for i in candidates]), spare
        for i in candidates:
            extra = min(most - holding[i], max(1, budget * weights[i] // whole), spare)
            holding[i] = holding[i] + extra
            spare = spare - extra
    return np.array([most] + holding)


def uneven_parts(own_key, number_of, total, reach, slope):
    if number_of == 2:
        one = jax.random.randint(own_key, (), max(1, total - reach), min(reach, total - 1) + 1)
        return jnp.stack([one, total - one])
    tallies = jnp.asarray(split_up(number_of, total, reach, slope), jnp.int32)
    twos = (number_of - 1) // 2
    giver, receiver = tallies[1:1 + 2 * twos:2], tallies[2:2 + 2 * twos:2]
    room = jnp.minimum(giver - 1, reach - receiver)
    shifted = jax.random.randint(jax.random.fold_in(own_key, 1), (twos,), 0, 1 << 20) % (room + 1)
    tallies = tallies.at[1:1 + 2 * twos:2].set(giver - shifted).at[2:2 + 2 * twos:2].set(receiver + shifted)
    return tallies[jax.random.permutation(jax.random.fold_in(own_key, 2), number_of)]


def bell_draw(rng, extent, scale, bound, cuts=(), kind=jnp.bfloat16):
    array = scale * jax.random.normal(rng, extent, jnp.float32)
    if cuts:
        array = array * block_scale(rng, extent, cuts, -0.22, 0.18)
    return jnp.clip(array, -bound, bound).astype(kind)


def setup_inputs(seed: int = 0) -> dict:
    arg_keys = jax.random.split(jax.random.key(seed), 5)
    hidden = draw_hidden(jax.random.fold_in(arg_keys[4], 71), 0)
    cotangent = draw_cotangent(jax.random.fold_in(arg_keys[4], 71), 0)
    w_down = bell_draw(arg_keys[2], (FF, D), FF ** -0.5, 0.046875, ((0, 8), (1, 4)))
    lengths = uneven_parts(arg_keys[3], BATCH, BATCH * SEQ * 3 // 4, SEQ, 1).astype(jnp.int32)
    return {"hidden": hidden, "cotangent": cotangent, "w_down": w_down, "lengths": lengths}


def reference(hidden, cotangent, w_down, lengths):
    positions = jnp.arange(SEQ, dtype=jnp.int32)
    keep = positions[None, :] < lengths[:, None]
    masked = jnp.where(keep[:, :, None], cotangent, jnp.zeros((), cotangent.dtype))
    flat = masked.reshape(BATCH * SEQ, D)
    d_hidden = jnp.dot(flat, w_down.T, preferred_element_type=jnp.float32).astype(jnp.bfloat16)
    d_hidden = d_hidden.reshape(BATCH, SEQ, FF)
    hid_f = hidden.astype(jnp.float32)
    cot_f = masked.astype(jnp.float32)
    hid_gram = jnp.einsum('bsf,btf->bst', hid_f, hid_f, precision=lax.Precision.HIGHEST)
    cot_gram = jnp.einsum('bsd,btd->bst', cot_f, cot_f, precision=lax.Precision.HIGHEST)
    sq_norm = lax.optimization_barrier(jnp.sum(hid_gram * cot_gram, axis=(1, 2)))
    radius = math.sqrt(FF * D / BATCH)
    clip_scale = radius / jnp.sqrt(sq_norm + 1e-06)
    weight_grad = jnp.einsum('bsf,bsd->fd', hid_f, cot_f * clip_scale[:, None, None], precision=lax.Precision.HIGHEST)
    return (weight_grad, d_hidden)
```

```python
import math

import jax
import jax.numpy as jnp
from jax import lax
from jax.sharding import PartitionSpec as P

F32 = jnp.float32
BF16 = jnp.bfloat16


def total_over(value, axis):
    size = lax.axis_size(axis)
    if size & (size - 1):
        return lax.psum(value, axis)
    step = 1
    while step < size:
        value = value + lax.ppermute(value, axis, [(i, i ^ step) for i in range(size)])
        step *= 2
    return value


def pieces(extent, count):
    while extent % (count * 128):
        count -= 1
        if count == 1:
            break
    size = extent // count
    return [(i * size, (i + 1) * size) for i in range(count)]


def body(hidden, cotangent, w_down, lengths):
    seqs, chunk, width = cotangent.shape
    units = hidden.shape[2]
    groups = lax.axis_size("dp")
    ranks = lax.axis_size("mp")
    seq_len = chunk * ranks
    share = width // groups
    inner = 2 if groups % 2 == 0 else 1
    outer = groups // inner
    me = lax.axis_index("dp")
    row, col = me // inner, me % inner

    def along_inner(value, k):
        perm = [(r * inner + c, r * inner + (c + k) % inner) for r in range(outer) for c in range(inner)]
        return lax.ppermute(value, "dp", perm)

    def along_outer(value, m):
        perm = [(r * inner + c, (r + m) % outer * inner + c) for r in range(outer) for c in range(inner)]
        return lax.ppermute(value, "dp", perm)

    def columns_of(c):
        blocks = [
            lax.dynamic_slice_in_dim(cotangent, ((row - m) % outer * inner + c) * share, share, 2)
            for m in range(outer)
        ]
        return jnp.concatenate(blocks, axis=2)

    cot_parts = [columns_of(col)]
    for k in range(1, inner):
        cot_parts.append(along_inner(columns_of((col + k) % inner), k))
    held, *cot_parts = lax.optimization_barrier((hidden, *cot_parts))

    w_parts = [w_down] + [along_outer(w_down, m) for m in range(1, outer)]
    hid_parts = [hidden] + [along_inner(held, k) for k in range(1, inner)]
    len_parts = [lengths] + [along_inner(lengths, k) for k in range(1, inner)]

    positions = jnp.arange(seq_len, dtype=jnp.int32)

    def masked_by(value, keep):
        return jnp.where(keep[:, :, None], value, jnp.zeros((), value.dtype))

    keeps = [positions[None, :] < n[:, None] for n in len_parts]

    slim = lax.all_to_all(cotangent, "mp", split_axis=2, concat_axis=1, tiled=True)
    slim = masked_by(slim, keeps[0])
    cot_gram = total_over(jnp.einsum("bsd,btd->bst", slim, slim, preferred_element_type=F32), "mp")
    hid_gram = jnp.einsum("bsf,btf->bst", hidden, hidden, preferred_element_type=F32)
    sq_norm = total_over(jnp.sum(hid_gram * cot_gram, axis=(1, 2)), "mp")
    radius = math.sqrt(units * ranks * width / (seqs * groups))
    clip = radius / jnp.sqrt(sq_norm + 1e-06)
    clips = [clip] + [along_inner(clip, k) for k in range(1, inner)]

    whole = lax.all_gather(jnp.stack(cot_parts), "mp", axis=2, tiled=True)
    masked = [masked_by(whole[k], keeps[k]) for k in range(inner)]
    tokens = seqs * seq_len

    def grad_w(m, lo, hi):
        total = None
        for k in range(inner):
            part = masked[k][:, :, m * share:(m + 1) * share]
            scaled = (part.astype(F32) * clips[k][:, None, None]).astype(BF16)
            term = lax.dot_general(
                hid_parts[k][:, :, lo:hi].reshape(tokens, hi - lo),
                scaled.reshape(tokens, share),
                (((0,), (0,)), ((), ())),
                preferred_element_type=F32,
            )
            total = term if total is None else total + term
        return total

    def grad_h(k, lo, hi):
        total = None
        for m in range(outer):
            term = lax.dot_general(
                masked[k][:, :, m * share:(m + 1) * share].reshape(tokens, share),
                w_parts[m][lo:hi],
                (((1,), (1,)), ((), ())),
                preferred_element_type=F32,
            )
            total = term if total is None else total + term
        return total

    cuts = pieces(units, 3)
    grad_w_in = [[along_outer(grad_w(m, *cut).astype(BF16), -m) for m in range(1, outer)] for cut in cuts]
    grad_h_in = [[along_inner(grad_h(k, *cut).astype(BF16), -k) for k in range(1, inner)] for cut in cuts]

    own_w, own_h = grad_w(0, 0, units), grad_h(0, 0, units)
    for k in range(inner - 1):
        own_h = own_h + jnp.concatenate([parts[k] for parts in grad_h_in], axis=1).astype(F32)
    for m in range(outer - 1):
        own_w = own_w + jnp.concatenate([parts[m] for parts in grad_w_in], axis=0).astype(F32)
    return (own_w, own_h.astype(BF16).reshape(seqs, seq_len, units))


def solution(mesh):
    in_specs = (P("dp", None, "mp"), P("dp", "mp", None), P("mp", "dp"), P("dp"))
    out_specs = (P("mp", "dp"), P("dp", None, "mp"))
    return jax.shard_map(body, mesh=mesh, in_specs=in_specs, out_specs=out_specs, check_vma=False)
```

```python
import functools
import math

import jax
import jax.numpy as jnp
from jax import lax
from jax.experimental import pallas as pl
from jax.experimental.layout import Layout, with_layout_constraint
from jax.experimental.pallas import tpu as pltpu
from jax.sharding import PartitionSpec as P

F32 = jnp.float32
BF16 = jnp.bfloat16


def total_over(value, axis):
    size = lax.axis_size(axis)
    if size & (size - 1):
        return lax.psum(value, axis)
    step = 1
    while step < size:
        value = value + lax.ppermute(value, axis, [(i, i ^ step) for i in range(size)])
        step *= 2
    return value


def pieces(extent, count):
    while extent % (count * 128):
        count -= 1
        if count == 1:
            break
    size = extent // count
    return [(i * size, (i + 1) * size) for i in range(count)]


def exchange_kernel(ranks, cot, hid, w, whole, hid_in, w_in, prod, hid_v, cot_v, gram_h, gram_out, gram_in,
                    local_sem, x_send, x_recv, big_send, big_recv, line_send, line_recv, core_send, core_recv,
                    gram_send, gram_recv, load_sem):
    seqs, chunk, _ = cot.shape
    share = w.shape[1]
    line = ranks // 2
    dp, mp = lax.axis_index("dp"), lax.axis_index("mp")
    row, col = dp // 2, dp % 2
    place, core = mp // 2, mp % 2
    across = {"dp": row * 2 + (1 - col)}
    along = {"dp": (1 - row) * 2 + col}
    sibling = {"mp": place * 2 + (1 - core)}
    right, left = {"mp": mp + 2}, {"mp": mp - 2}
    has_right, has_left = place < line - 1, place > 0

    barrier = pltpu.get_barrier_semaphore()
    for device in (across, along, sibling):
        pl.semaphore_signal(barrier, inc=1, device_id=device, device_id_type=pl.DeviceIdType.MESH)

    @pl.when(has_right)
    def _():
        pl.semaphore_signal(barrier, inc=1, device_id=right, device_id_type=pl.DeviceIdType.MESH)

    @pl.when(has_left)
    def _():
        pl.semaphore_signal(barrier, inc=1, device_id=left, device_id_type=pl.DeviceIdType.MESH)

    pl.semaphore_wait(barrier, 3 + jnp.where(has_right, 1, 0) + jnp.where(has_left, 1, 0))

    def remote(src, dst, send, recv, device):
        return pltpu.make_async_remote_copy(
            src_ref=src, dst_ref=dst, send_sem=send, recv_sem=recv, device_id=device,
            device_id_type=pl.DeviceIdType.MESH)

    def slot(k, at, kore):
        rows = pl.ds(pl.multiple_of((at * 2 + kore) * chunk, chunk), chunk)
        return whole.at[pl.ds(k * seqs, seqs), rows, :]

    def columns(m, c):
        start = pl.multiple_of(((row + m) % 2 * 2 + c) * share, share)
        return cot.at[:, :, pl.ds(start, share)]

    def target(k, m):
        rows = pl.ds(pl.multiple_of(mp * chunk, chunk), chunk)
        return whole.at[pl.ds(k * seqs, seqs), rows, pl.ds(m * share, share)]

    own = [pltpu.make_async_copy(columns(m, col), target(0, m), local_sem.at[m]) for m in range(2)]
    over = [remote(columns(m, 1 - col), target(1, m), x_send.at[m], x_recv.at[m], across) for m in range(2)]
    big = [remote(w, w_in, big_send.at[0], big_recv.at[0], along),
           remote(hid, hid_in, big_send.at[1], big_recv.at[1], across)]
    load_h = pltpu.make_async_copy(hid, hid_v, load_sem.at[0])
    for copy in (*own, *over, *big, load_h):
        copy.start()

    def to_right(k, s):
        return remote(slot(k, place - s, core), slot(k, place - s, core),
                      line_send.at[k, 0, s], line_recv.at[k, 0, s], right)

    def to_left(k, s):
        return remote(slot(k, place + s, core), slot(k, place + s, core),
                      line_send.at[k, 1, s], line_recv.at[k, 1, s], left)

    def to_core(k, at):
        return remote(slot(k, at, core), slot(k, at, core),
                      core_send.at[k, at], core_recv.at[k, at], sibling)

    def gram(ref, b):
        value = ref[b]
        return lax.dot_general(value, value, (((1,), (1,)), ((), ())), preferred_element_type=F32)

    for k in range(2):
        for copy in (own if k == 0 else over):
            copy.wait()

        @pl.when(has_right)
        def _(k=k):
            to_right(k, 0).start()

        @pl.when(has_left)
        def _(k=k):
            to_left(k, 0).start()

        to_core(k, place).start()
        if k == 0:
            continue
        load_h.wait()

        @pl.loop(0, seqs)
        def _(b):
            gram_h[b] = gram(hid_v, b)

    for s in range(1, line):
        for k in range(2):
            @pl.when(place - s >= 0)
            def _(k=k, s=s):
                remote(slot(k, place - s, core), slot(k, place - s, core),
                       line_send.at[k, 0, s - 1], line_recv.at[k, 0, s - 1], right).wait_recv()

                @pl.when(has_right)
                def _():
                    to_right(k, s).start()

                to_core(k, place - s).start()

            @pl.when(place + s < line)
            def _(k=k, s=s):
                remote(slot(k, place + s, core), slot(k, place + s, core),
                       line_send.at[k, 1, s - 1], line_recv.at[k, 1, s - 1], left).wait_recv()

                @pl.when(has_left)
                def _():
                    to_left(k, s).start()

                to_core(k, place + s).start()

    def arrive(k):
        for at in range(line):
            remote(slot(k, at, 1 - core), slot(k, at, 1 - core),
                   core_send.at[k, at], core_recv.at[k, at], sibling).wait_recv()
        load = pltpu.make_async_copy(whole.at[pl.ds(k * seqs, seqs)], cot_v, load_sem.at[1])
        load.start()
        load.wait()

    arrive(1)

    @pl.loop(0, seqs)
    def _(b):
        gram_out[b] = gram(cot_v, b)

    sums = remote(gram_out, gram_in, gram_send, gram_recv, across)
    sums.start()
    arrive(0)
    sums.wait_recv()

    @pl.loop(0, seqs)
    def _(b):
        gram_h[b] = gram_h[b] * (gram(cot_v, b) + gram_in[b])

    result = pltpu.make_async_copy(gram_h, prod, load_sem.at[2])
    result.start()
    sums.wait_send()
    for k in range(2):
        for at in range(line):
            to_core(k, at).wait_send()
        for s in range(line - 1):
            @pl.when(has_right & (place - s >= 0))
            def _(k=k, s=s):
                to_right(k, s).wait_send()

            @pl.when(has_left & (place + s < line))
            def _(k=k, s=s):
                to_left(k, s).wait_send()
    result.wait()
    for copy in big:
        copy.wait()


def exchange(cotangent, hidden, w_down):
    seqs, chunk, _ = cotangent.shape
    ranks = lax.axis_size("mp")
    share = w_down.shape[1]
    line = ranks // 2
    seq_len = chunk * ranks
    dma = pltpu.SemaphoreType.DMA
    square = (seqs, seq_len, seq_len)
    anywhere = pl.BlockSpec(memory_space=pl.ANY)
    return pl.pallas_call(
        functools.partial(exchange_kernel, ranks),
        out_shape=(
            jax.ShapeDtypeStruct((2 * seqs, seq_len, 2 * share), BF16),
            jax.ShapeDtypeStruct(hidden.shape, BF16),
            jax.ShapeDtypeStruct(w_down.shape, BF16),
            jax.ShapeDtypeStruct(square, F32),
        ),
        in_specs=[anywhere] * 3,
        out_specs=(anywhere,) * 4,
        scratch_shapes=[
            pltpu.VMEM(hidden.shape, BF16),
            pltpu.VMEM((seqs, seq_len, 2 * share), BF16),
            pltpu.VMEM(square, F32),
            pltpu.VMEM(square, F32),
            pltpu.VMEM(square, F32),
            dma((2,)), dma((2,)), dma((2,)), dma((2,)), dma((2,)),
            dma((2, 2, line)), dma((2, 2, line)), dma((2, line)), dma((2, line)),
            dma, dma, dma((3,)),
        ],
        compiler_params=pltpu.CompilerParams(
            collective_id=0, has_side_effects=True, vmem_limit_bytes=48 * 1024 * 1024),
    )(cotangent, hidden, w_down)


def body(hidden, cotangent, w_down, lengths):
    seqs, chunk, width = cotangent.shape
    units = hidden.shape[2]
    groups = lax.axis_size("dp")
    ranks = lax.axis_size("mp")
    seq_len = chunk * ranks
    share = width // groups
    inner = 2 if groups % 2 == 0 else 1
    outer = groups // inner
    me = lax.axis_index("dp")
    row, col = me // inner, me % inner

    def along_inner(value, k):
        perm = [(r * inner + c, r * inner + (c + k) % inner) for r in range(outer) for c in range(inner)]
        return lax.ppermute(value, "dp", perm)

    def along_outer(value, m):
        perm = [(r * inner + c, (r + m) % outer * inner + c) for r in range(outer) for c in range(inner)]
        return lax.ppermute(value, "dp", perm)

    len_parts = [lengths] + [along_inner(lengths, k) for k in range(1, inner)]

    positions = jnp.arange(seq_len, dtype=jnp.int32)

    def masked_by(value, keep):
        return jnp.where(keep[:, :, None], value, jnp.zeros((), value.dtype))

    keeps = [positions[None, :] < n[:, None] for n in len_parts]

    if (inner, outer) == (2, 2) and ranks % 2 == 0 and chunk % 16 == 0 and share % 128 == 0:
        whole, hid_in, w_in, prod = exchange(cotangent, hidden, w_down)
        whole = whole.reshape(inner, seqs, seq_len, inner * share)
        w_parts, hid_parts = [w_down, w_in], [hidden, hid_in]
        both = keeps[0][:, :, None] & keeps[0][:, None, :]
        sq_norm = total_over(jnp.sum(jnp.where(both, prod, 0.0), axis=(1, 2)), "mp")
    else:
        def columns_of(c):
            blocks = [
                lax.dynamic_slice_in_dim(cotangent, ((row - m) % outer * inner + c) * share, share, 2)
                for m in range(outer)
            ]
            return jnp.concatenate(blocks, axis=2)

        cot_parts = [columns_of(col)]
        for k in range(1, inner):
            cot_parts.append(along_inner(columns_of((col + k) % inner), k))
        held, *cot_parts = lax.optimization_barrier((hidden, *cot_parts))

        w_parts = [w_down] + [along_outer(w_down, m) for m in range(1, outer)]
        hid_parts = [hidden] + [along_inner(held, k) for k in range(1, inner)]
        slim = lax.all_to_all(cotangent, "mp", split_axis=2, concat_axis=1, tiled=True)
        slim = masked_by(slim, keeps[0])
        cot_gram = total_over(jnp.einsum("bsd,btd->bst", slim, slim, preferred_element_type=F32), "mp")
        hid_gram = jnp.einsum("bsf,btf->bst", hidden, hidden, preferred_element_type=F32)
        sq_norm = total_over(jnp.sum(hid_gram * cot_gram, axis=(1, 2)), "mp")
        whole = lax.all_gather(jnp.stack(cot_parts), "mp", axis=2, tiled=True)
    radius = math.sqrt(units * ranks * width / (seqs * groups))
    clip = radius / jnp.sqrt(sq_norm + 1e-06)
    clips = [clip] + [along_inner(clip, k) for k in range(1, inner)]

    masked = [masked_by(whole[k], keeps[k]) for k in range(inner)]
    tokens = seqs * seq_len

    def grad_w(m, lo, hi):
        total = None
        for k in range(inner):
            part = masked[k][:, :, m * share:(m + 1) * share]
            scaled = (part.astype(F32) * clips[k][:, None, None]).astype(BF16)
            term = lax.dot_general(
                hid_parts[k][:, :, lo:hi].reshape(tokens, hi - lo),
                scaled.reshape(tokens, share),
                (((0,), (0,)), ((), ())),
                preferred_element_type=F32,
            )
            total = term if total is None else total + term
        return total

    def grad_h(k, lo, hi):
        total = None
        for m in range(outer):
            term = lax.dot_general(
                masked[k][:, :, m * share:(m + 1) * share].reshape(tokens, share),
                w_parts[m][lo:hi],
                (((1,), (1,)), ((), ())),
                preferred_element_type=F32,
            )
            total = term if total is None else total + term
        return total

    cuts = pieces(units, 3)
    grad_w_in = [[along_outer(grad_w(m, *cut).astype(BF16), -m) for m in range(1, outer)] for cut in cuts]
    grad_h_in = [[along_inner(grad_h(k, *cut).astype(BF16), -k) for k in range(1, inner)] for cut in cuts]

    own_w, own_h = lax.optimization_barrier((grad_w(0, 0, units), grad_h(0, 0, units)))
    own_w = with_layout_constraint(own_w, Layout(major_to_minor=(0, 1)))
    for k in range(inner - 1):
        own_h = own_h + jnp.concatenate([parts[k] for parts in grad_h_in], axis=1).astype(F32)
    for m in range(outer - 1):
        own_w = own_w + jnp.concatenate([parts[m] for parts in grad_w_in], axis=0).astype(F32)
    return (own_w, own_h.astype(BF16).reshape(seqs, seq_len, units))


def solution(mesh):
    in_specs = (P("dp", None, "mp"), P("dp", "mp", None), P("mp", "dp"), P("dp"))
    out_specs = (P("mp", "dp"), P("dp", None, "mp"))
    return jax.shard_map(body, mesh=mesh, in_specs=in_specs, out_specs=out_specs, check_vma=False)
```

```python
import functools
import math

import jax
import jax.numpy as jnp
from jax import lax
from jax.experimental import pallas as pl
from jax.experimental.layout import Layout, with_layout_constraint
from jax.experimental.pallas import tpu as pltpu
from jax.sharding import PartitionSpec as P

F32 = jnp.float32
BF16 = jnp.bfloat16


def total_over(value, axis):
    size = lax.axis_size(axis)
    if size & (size - 1):
        return lax.psum(value, axis)
    step = 1
    while step < size:
        value = value + lax.ppermute(value, axis, [(i, i ^ step) for i in range(size)])
        step *= 2
    return value


def pieces(extent, count):
    while extent % (count * 128):
        count -= 1
        if count == 1:
            break
    size = extent // count
    return [(i * size, (i + 1) * size) for i in range(count)]


def exchange_kernel(ranks, cot, hid, w, whole, hid_in, w_in, prod, hid_v, cot_v, gram_h, gram_out, gram_in,
                    local_sem, x_send, x_recv, big_send, big_recv, line_send, line_recv, core_send, core_recv,
                    gram_send, gram_recv, load_sem):
    seqs, chunk, _ = cot.shape
    share = w.shape[1]
    line = ranks // 2
    dp, mp = lax.axis_index("dp"), lax.axis_index("mp")
    row, col = dp // 2, dp % 2
    place, core = mp // 2, mp % 2
    across = {"dp": row * 2 + (1 - col)}
    along = {"dp": (1 - row) * 2 + col}
    sibling = {"mp": place * 2 + (1 - core)}
    right, left = {"mp": mp + 2}, {"mp": mp - 2}
    has_right, has_left = place < line - 1, place > 0

    barrier = pltpu.get_barrier_semaphore()
    for device in (across, along, sibling):
        pl.semaphore_signal(barrier, inc=1, device_id=device, device_id_type=pl.DeviceIdType.MESH)

    @pl.when(has_right)
    def _():
        pl.semaphore_signal(barrier, inc=1, device_id=right, device_id_type=pl.DeviceIdType.MESH)

    @pl.when(has_left)
    def _():
        pl.semaphore_signal(barrier, inc=1, device_id=left, device_id_type=pl.DeviceIdType.MESH)

    pl.semaphore_wait(barrier, 3 + jnp.where(has_right, 1, 0) + jnp.where(has_left, 1, 0))

    def remote(src, dst, send, recv, device):
        return pltpu.make_async_remote_copy(
            src_ref=src, dst_ref=dst, send_sem=send, recv_sem=recv, device_id=device,
            device_id_type=pl.DeviceIdType.MESH)

    def slot(k, at, kore):
        rows = pl.ds(pl.multiple_of((at * 2 + kore) * chunk, chunk), chunk)
        return whole.at[pl.ds(k * seqs, seqs), rows, :]

    def columns(m, c):
        start = pl.multiple_of(((row + m) % 2 * 2 + c) * share, share)
        return cot.at[:, :, pl.ds(start, share)]

    def target(k, m):
        rows = pl.ds(pl.multiple_of(mp * chunk, chunk), chunk)
        return whole.at[pl.ds(k * seqs, seqs), rows, pl.ds(m * share, share)]

    own = [pltpu.make_async_copy(columns(m, col), target(0, m), local_sem.at[m]) for m in range(2)]
    over = [remote(columns(m, 1 - col), target(1, m), x_send.at[m], x_recv.at[m], across) for m in range(2)]
    big = [remote(w, w_in, big_send.at[0], big_recv.at[0], along),
           remote(hid, hid_in, big_send.at[1], big_recv.at[1], across)]
    load_h = pltpu.make_async_copy(hid, hid_v, load_sem.at[0])
    for copy in (*own, *over, *big, load_h):
        copy.start()

    def to_right(k, s):
        return remote(slot(k, place - s, core), slot(k, place - s, core),
                      line_send.at[k, 0, s], line_recv.at[k, 0, s], right)

    def to_left(k, s):
        return remote(slot(k, place + s, core), slot(k, place + s, core),
                      line_send.at[k, 1, s], line_recv.at[k, 1, s], left)

    def to_core(k, at):
        return remote(slot(k, at, core), slot(k, at, core),
                      core_send.at[k, at], core_recv.at[k, at], sibling)

    def gram(ref, b):
        value = ref[b]
        return lax.dot_general(value, value, (((1,), (1,)), ((), ())), preferred_element_type=F32)

    for k in range(2):
        for copy in (own if k == 0 else over):
            copy.wait()

        @pl.when(has_right)
        def _(k=k):
            to_right(k, 0).start()

        @pl.when(has_left)
        def _(k=k):
            to_left(k, 0).start()

        to_core(k, place).start()
        if k == 0:
            continue
        load_h.wait()

        @pl.loop(0, seqs)
        def _(b):
            gram_h[b] = gram(hid_v, b)

    for s in range(1, line):
        for k in range(2):
            @pl.when(place - s >= 0)
            def _(k=k, s=s):
                remote(slot(k, place - s, core), slot(k, place - s, core),
                       line_send.at[k, 0, s - 1], line_recv.at[k, 0, s - 1], right).wait_recv()

                @pl.when(has_right)
                def _():
                    to_right(k, s).start()

                to_core(k, place - s).start()

            @pl.when(place + s < line)
            def _(k=k, s=s):
                remote(slot(k, place + s, core), slot(k, place + s, core),
                       line_send.at[k, 1, s - 1], line_recv.at[k, 1, s - 1], left).wait_recv()

                @pl.when(has_left)
                def _():
                    to_left(k, s).start()

                to_core(k, place + s).start()

    def arrive(k):
        for at in range(line):
            remote(slot(k, at, 1 - core), slot(k, at, 1 - core),
                   core_send.at[k, at], core_recv.at[k, at], sibling).wait_recv()
        load = pltpu.make_async_copy(whole.at[pl.ds(k * seqs, seqs)], cot_v, load_sem.at[1])
        load.start()
        load.wait()

    arrive(1)

    @pl.loop(0, seqs)
    def _(b):
        gram_out[b] = gram(cot_v, b)

    sums = remote(gram_out, gram_in, gram_send, gram_recv, across)
    sums.start()
    arrive(0)
    sums.wait_recv()

    @pl.loop(0, seqs)
    def _(b):
        gram_h[b] = gram_h[b] * (gram(cot_v, b) + gram_in[b])

    result = pltpu.make_async_copy(gram_h, prod, load_sem.at[2])
    result.start()
    sums.wait_send()
    for k in range(2):
        for at in range(line):
            to_core(k, at).wait_send()
        for s in range(line - 1):
            @pl.when(has_right & (place - s >= 0))
            def _(k=k, s=s):
                to_right(k, s).wait_send()

            @pl.when(has_left & (place + s < line))
            def _(k=k, s=s):
                to_left(k, s).wait_send()
    result.wait()
    for copy in big:
        copy.wait()


def exchange(cotangent, hidden, w_down):
    seqs, chunk, _ = cotangent.shape
    ranks = lax.axis_size("mp")
    share = w_down.shape[1]
    line = ranks // 2
    seq_len = chunk * ranks
    dma = pltpu.SemaphoreType.DMA
    square = (seqs, seq_len, seq_len)
    anywhere = pl.BlockSpec(memory_space=pl.ANY)
    return pl.pallas_call(
        functools.partial(exchange_kernel, ranks),
        out_shape=(
            jax.ShapeDtypeStruct((2 * seqs, seq_len, 2 * share), BF16),
            jax.ShapeDtypeStruct(hidden.shape, BF16),
            jax.ShapeDtypeStruct(w_down.shape, BF16),
            jax.ShapeDtypeStruct(square, F32),
        ),
        in_specs=[anywhere] * 3,
        out_specs=(anywhere,) * 4,
        scratch_shapes=[
            pltpu.VMEM(hidden.shape, BF16),
            pltpu.VMEM((seqs, seq_len, 2 * share), BF16),
            pltpu.VMEM(square, F32),
            pltpu.VMEM(square, F32),
            pltpu.VMEM(square, F32),
            dma((2,)), dma((2,)), dma((2,)), dma((2,)), dma((2,)),
            dma((2, 2, line)), dma((2, 2, line)), dma((2, line)), dma((2, line)),
            dma, dma, dma((3,)),
        ],
        compiler_params=pltpu.CompilerParams(
            collective_id=0, has_side_effects=True, vmem_limit_bytes=48 * 1024 * 1024),
    )(cotangent, hidden, w_down)


def body(hidden, cotangent, w_down, lengths):
    seqs, chunk, width = cotangent.shape
    units = hidden.shape[2]
    groups = lax.axis_size("dp")
    ranks = lax.axis_size("mp")
    seq_len = chunk * ranks
    share = width // groups
    inner = 2 if groups % 2 == 0 else 1
    outer = groups // inner
    me = lax.axis_index("dp")
    row, col = me // inner, me % inner

    def along_inner(value, k):
        perm = [(r * inner + c, r * inner + (c + k) % inner) for r in range(outer) for c in range(inner)]
        return lax.ppermute(value, "dp", perm)

    def along_outer(value, m):
        perm = [(r * inner + c, (r + m) % outer * inner + c) for r in range(outer) for c in range(inner)]
        return lax.ppermute(value, "dp", perm)

    len_parts = [lengths] + [along_inner(lengths, k) for k in range(1, inner)]

    positions = jnp.arange(seq_len, dtype=jnp.int32)

    def masked_by(value, keep):
        return jnp.where(keep[:, :, None], value, jnp.zeros((), value.dtype))

    keeps = [positions[None, :] < n[:, None] for n in len_parts]

    if (inner, outer) == (2, 2) and ranks % 2 == 0 and chunk % 16 == 0 and share % 128 == 0:
        whole, hid_in, w_in, prod = exchange(cotangent, hidden, w_down)
        whole = whole.reshape(inner, seqs, seq_len, inner * share)
        w_parts, hid_parts = [w_down, w_in], [hidden, hid_in]
        both = keeps[0][:, :, None] & keeps[0][:, None, :]
        sq_norm = total_over(jnp.sum(jnp.where(both, prod, 0.0), axis=(1, 2)), "mp")
    else:
        def columns_of(c):
            blocks = [
                lax.dynamic_slice_in_dim(cotangent, ((row - m) % outer * inner + c) * share, share, 2)
                for m in range(outer)
            ]
            return jnp.concatenate(blocks, axis=2)

        cot_parts = [columns_of(col)]
        for k in range(1, inner):
            cot_parts.append(along_inner(columns_of((col + k) % inner), k))
        held, *cot_parts = lax.optimization_barrier((hidden, *cot_parts))

        w_parts = [w_down] + [along_outer(w_down, m) for m in range(1, outer)]
        hid_parts = [hidden] + [along_inner(held, k) for k in range(1, inner)]
        slim = lax.all_to_all(cotangent, "mp", split_axis=2, concat_axis=1, tiled=True)
        slim = masked_by(slim, keeps[0])
        cot_gram = total_over(jnp.einsum("bsd,btd->bst", slim, slim, preferred_element_type=F32), "mp")
        hid_gram = jnp.einsum("bsf,btf->bst", hidden, hidden, preferred_element_type=F32)
        sq_norm = total_over(jnp.sum(hid_gram * cot_gram, axis=(1, 2)), "mp")
        whole = lax.all_gather(jnp.stack(cot_parts), "mp", axis=2, tiled=True)
    radius = math.sqrt(units * ranks * width / (seqs * groups))
    clip = radius / jnp.sqrt(sq_norm + 1e-06)
    clips = [clip] + [along_inner(clip, k) for k in range(1, inner)]

    whole, *clips = lax.optimization_barrier((whole, *clips))
    masked = [masked_by(whole[k], keeps[k]) for k in range(inner)]
    tokens = seqs * seq_len

    def grad_w(m, lo, hi):
        total = None
        for k in range(inner):
            part = masked[k][:, :, m * share:(m + 1) * share]
            scaled = (part.astype(F32) * clips[k][:, None, None]).astype(BF16)
            term = lax.dot_general(
                hid_parts[k][:, :, lo:hi].reshape(tokens, hi - lo),
                scaled.reshape(tokens, share),
                (((0,), (0,)), ((), ())),
                preferred_element_type=F32,
            )
            total = term if total is None else total + term
        return total

    def grad_h(source, lo, hi):
        total = None
        for m in range(outer):
            term = lax.dot_general(
                source[:, :, m * share:(m + 1) * share].reshape(tokens, share),
                w_parts[m][lo:hi],
                (((1,), (1,)), ((), ())),
                preferred_element_type=F32,
            )
            total = term if total is None else total + term
        return total

    cuts = pieces(units, 3)
    w_terms = [[grad_w(m, *cut).astype(BF16) for m in range(1, outer)] for cut in cuts]
    grad_w_in = [[along_outer(terms[m - 1], -m) for m in range(1, outer)] for terms in w_terms]
    others, w_terms[0] = lax.optimization_barrier((masked[1:], w_terms[0]))
    grad_h_in = [
        [along_inner(grad_h(others[k - 1], *cut).astype(BF16), -k) for k in range(1, inner)] for cut in cuts
    ]

    own_w, own_h = lax.optimization_barrier((grad_w(0, 0, units), grad_h(masked[0], 0, units)))
    own_w = with_layout_constraint(own_w, Layout(major_to_minor=(0, 1)))
    for k in range(inner - 1):
        own_h = own_h + jnp.concatenate([parts[k] for parts in grad_h_in], axis=1).astype(F32)
    for m in range(outer - 1):
        own_w = own_w + jnp.concatenate([parts[m] for parts in grad_w_in], axis=0).astype(F32)
    return (own_w, own_h.astype(BF16).reshape(seqs, seq_len, units))


def solution(mesh):
    in_specs = (P("dp", None, "mp"), P("dp", "mp", None), P("mp", "dp"), P("dp"))
    out_specs = (P("mp", "dp"), P("dp", None, "mp"))
    return jax.shard_map(body, mesh=mesh, in_specs=in_specs, out_specs=out_specs, check_vma=False)
```

```python
import functools
import math

import jax
import jax.numpy as jnp
from jax import lax
from jax.experimental import pallas as pl
from jax.experimental.layout import Layout, with_layout_constraint
from jax.experimental.pallas import tpu as pltpu
from jax.sharding import PartitionSpec as P

F32 = jnp.float32
BF16 = jnp.bfloat16


def total_over(value, axis):
    size = lax.axis_size(axis)
    if size & (size - 1):
        return lax.psum(value, axis)
    step = 1
    while step < size:
        value = value + lax.ppermute(value, axis, [(i, i ^ step) for i in range(size)])
        step *= 2
    return value


def pieces(extent, count):
    while extent % (count * 128):
        count -= 1
        if count == 1:
            break
    size = extent // count
    return [(i * size, (i + 1) * size) for i in range(count)]


def exchange_kernel(ranks, cot, hid, w, whole, hid_in, w_in, prod, hid_v, cot_v, gram_h, gram_out, gram_in,
                    local_sem, x_send, x_recv, big_send, big_recv, line_send, line_recv, core_send, core_recv,
                    gram_send, gram_recv, load_sem):
    seqs, chunk, _ = cot.shape
    share = w.shape[1]
    line = ranks // 2
    dp, mp = lax.axis_index("dp"), lax.axis_index("mp")
    row, col = dp // 2, dp % 2
    place, core = mp // 2, mp % 2
    across = {"dp": row * 2 + (1 - col)}
    along = {"dp": (1 - row) * 2 + col}
    sibling = {"mp": place * 2 + (1 - core)}
    right, left = {"mp": mp + 2}, {"mp": mp - 2}
    has_right, has_left = place < line - 1, place > 0

    barrier = pltpu.get_barrier_semaphore()
    for device in (across, along, sibling):
        pl.semaphore_signal(barrier, inc=1, device_id=device, device_id_type=pl.DeviceIdType.MESH)

    @pl.when(has_right)
    def _():
        pl.semaphore_signal(barrier, inc=1, device_id=right, device_id_type=pl.DeviceIdType.MESH)

    @pl.when(has_left)
    def _():
        pl.semaphore_signal(barrier, inc=1, device_id=left, device_id_type=pl.DeviceIdType.MESH)

    pl.semaphore_wait(barrier, 3 + jnp.where(has_right, 1, 0) + jnp.where(has_left, 1, 0))

    def remote(src, dst, send, recv, device):
        return pltpu.make_async_remote_copy(
            src_ref=src, dst_ref=dst, send_sem=send, recv_sem=recv, device_id=device,
            device_id_type=pl.DeviceIdType.MESH)

    def slot(k, at, kore):
        rows = pl.ds(pl.multiple_of((at * 2 + kore) * chunk, chunk), chunk)
        return whole.at[pl.ds(k * seqs, seqs), rows, :]

    def columns(m, c):
        start = pl.multiple_of(((row + m) % 2 * 2 + c) * share, share)
        return cot.at[:, :, pl.ds(start, share)]

    def target(k, m):
        rows = pl.ds(pl.multiple_of(mp * chunk, chunk), chunk)
        return whole.at[pl.ds(k * seqs, seqs), rows, pl.ds(m * share, share)]

    own = [pltpu.make_async_copy(columns(m, col), target(0, m), local_sem.at[m]) for m in range(2)]
    over = [remote(columns(m, 1 - col), target(1, m), x_send.at[m], x_recv.at[m], across) for m in range(2)]
    big = [remote(w, w_in, big_send.at[0], big_recv.at[0], along),
           remote(hid, hid_in, big_send.at[1], big_recv.at[1], across)]
    load_h = pltpu.make_async_copy(hid, hid_v, load_sem.at[0])
    for copy in (*own, *over, *big, load_h):
        copy.start()

    def to_right(k, s):
        return remote(slot(k, place - s, core), slot(k, place - s, core),
                      line_send.at[k, 0, s], line_recv.at[k, 0, s], right)

    def to_left(k, s):
        return remote(slot(k, place + s, core), slot(k, place + s, core),
                      line_send.at[k, 1, s], line_recv.at[k, 1, s], left)

    def to_core(k, at):
        return remote(slot(k, at, core), slot(k, at, core),
                      core_send.at[k, at], core_recv.at[k, at], sibling)

    def gram(ref, b):
        value = ref[b]
        return lax.dot_general(value, value, (((1,), (1,)), ((), ())), preferred_element_type=F32)

    for k in range(2):
        for copy in (own if k == 0 else over):
            copy.wait()

        @pl.when(has_right)
        def _(k=k):
            to_right(k, 0).start()

        @pl.when(has_left)
        def _(k=k):
            to_left(k, 0).start()

        to_core(k, place).start()
        if k == 0:
            continue
        load_h.wait()

        @pl.loop(0, seqs)
        def _(b):
            gram_h[b] = gram(hid_v, b)

    for s in range(1, line):
        for k in range(2):
            @pl.when(place - s >= 0)
            def _(k=k, s=s):
                remote(slot(k, place - s, core), slot(k, place - s, core),
                       line_send.at[k, 0, s - 1], line_recv.at[k, 0, s - 1], right).wait_recv()

                @pl.when(has_right)
                def _():
                    to_right(k, s).start()

                to_core(k, place - s).start()

            @pl.when(place + s < line)
            def _(k=k, s=s):
                remote(slot(k, place + s, core), slot(k, place + s, core),
                       line_send.at[k, 1, s - 1], line_recv.at[k, 1, s - 1], left).wait_recv()

                @pl.when(has_left)
                def _():
                    to_left(k, s).start()

                to_core(k, place + s).start()

    def arrive(k):
        for at in range(line):
            remote(slot(k, at, 1 - core), slot(k, at, 1 - core),
                   core_send.at[k, at], core_recv.at[k, at], sibling).wait_recv()
        load = pltpu.make_async_copy(whole.at[pl.ds(k * seqs, seqs)], cot_v, load_sem.at[1])
        load.start()
        load.wait()

    arrive(1)

    @pl.loop(0, seqs)
    def _(b):
        gram_out[b] = gram(cot_v, b)

    sums = remote(gram_out, gram_in, gram_send, gram_recv, across)
    sums.start()
    arrive(0)
    sums.wait_recv()

    @pl.loop(0, seqs)
    def _(b):
        gram_h[b] = gram_h[b] * (gram(cot_v, b) + gram_in[b])

    result = pltpu.make_async_copy(gram_h, prod, load_sem.at[2])
    result.start()
    sums.wait_send()
    for k in range(2):
        for at in range(line):
            to_core(k, at).wait_send()
        for s in range(line - 1):
            @pl.when(has_right & (place - s >= 0))
            def _(k=k, s=s):
                to_right(k, s).wait_send()

            @pl.when(has_left & (place + s < line))
            def _(k=k, s=s):
                to_left(k, s).wait_send()
    result.wait()
    for copy in big:
        copy.wait()


def exchange(cotangent, hidden, w_down):
    seqs, chunk, _ = cotangent.shape
    ranks = lax.axis_size("mp")
    share = w_down.shape[1]
    line = ranks // 2
    seq_len = chunk * ranks
    dma = pltpu.SemaphoreType.DMA
    square = (seqs, seq_len, seq_len)
    anywhere = pl.BlockSpec(memory_space=pl.ANY)
    return pl.pallas_call(
        functools.partial(exchange_kernel, ranks),
        out_shape=(
            jax.ShapeDtypeStruct((2 * seqs, seq_len, 2 * share), BF16),
            jax.ShapeDtypeStruct(hidden.shape, BF16),
            jax.ShapeDtypeStruct(w_down.shape, BF16),
            jax.ShapeDtypeStruct(square, F32),
        ),
        in_specs=[anywhere] * 3,
        out_specs=(anywhere,) * 4,
        scratch_shapes=[
            pltpu.VMEM(hidden.shape, BF16),
            pltpu.VMEM((seqs, seq_len, 2 * share), BF16),
            pltpu.VMEM(square, F32),
            pltpu.VMEM(square, F32),
            pltpu.VMEM(square, F32),
            dma((2,)), dma((2,)), dma((2,)), dma((2,)), dma((2,)),
            dma((2, 2, line)), dma((2, 2, line)), dma((2, line)), dma((2, line)),
            dma, dma, dma((3,)),
        ],
        compiler_params=pltpu.CompilerParams(
            collective_id=0, has_side_effects=True, vmem_limit_bytes=48 * 1024 * 1024),
    )(cotangent, hidden, w_down)


def body(hidden, cotangent, w_down, lengths):
    seqs, chunk, width = cotangent.shape
    units = hidden.shape[2]
    groups = lax.axis_size("dp")
    ranks = lax.axis_size("mp")
    seq_len = chunk * ranks
    share = width // groups
    inner = 2 if groups % 2 == 0 else 1
    outer = groups // inner
    me = lax.axis_index("dp")
    row, col = me // inner, me % inner

    def along_inner(value, k):
        perm = [(r * inner + c, r * inner + (c + k) % inner) for r in range(outer) for c in range(inner)]
        return lax.ppermute(value, "dp", perm)

    def along_outer(value, m):
        perm = [(r * inner + c, (r + m) % outer * inner + c) for r in range(outer) for c in range(inner)]
        return lax.ppermute(value, "dp", perm)

    len_parts = [lengths] + [along_inner(lengths, k) for k in range(1, inner)]

    positions = jnp.arange(seq_len, dtype=jnp.int32)

    def masked_by(value, keep):
        return jnp.where(keep[:, :, None], value, jnp.zeros((), value.dtype))

    keeps = [positions[None, :] < n[:, None] for n in len_parts]

    if (inner, outer) == (2, 2) and ranks % 2 == 0 and chunk % 16 == 0 and share % 128 == 0:
        whole, hid_in, w_in, prod = exchange(cotangent, hidden, w_down)
        whole = whole.reshape(inner, seqs, seq_len, inner * share)
        w_parts, hid_parts = [w_down, w_in], [hidden, hid_in]
        both = keeps[0][:, :, None] & keeps[0][:, None, :]
        sq_norm = total_over(jnp.sum(jnp.where(both, prod, 0.0), axis=(1, 2)), "mp")
    else:
        def columns_of(c):
            blocks = [
                lax.dynamic_slice_in_dim(cotangent, ((row - m) % outer * inner + c) * share, share, 2)
                for m in range(outer)
            ]
            return jnp.concatenate(blocks, axis=2)

        cot_parts = [columns_of(col)]
        for k in range(1, inner):
            cot_parts.append(along_inner(columns_of((col + k) % inner), k))
        held, *cot_parts = lax.optimization_barrier((hidden, *cot_parts))

        w_parts = [w_down] + [along_outer(w_down, m) for m in range(1, outer)]
        hid_parts = [hidden] + [along_inner(held, k) for k in range(1, inner)]
        slim = lax.all_to_all(cotangent, "mp", split_axis=2, concat_axis=1, tiled=True)
        slim = masked_by(slim, keeps[0])
        cot_gram = total_over(jnp.einsum("bsd,btd->bst", slim, slim, preferred_element_type=F32), "mp")
        hid_gram = jnp.einsum("bsf,btf->bst", hidden, hidden, preferred_element_type=F32)
        sq_norm = total_over(jnp.sum(hid_gram * cot_gram, axis=(1, 2)), "mp")
        whole = lax.all_gather(jnp.stack(cot_parts), "mp", axis=2, tiled=True)
    radius = math.sqrt(units * ranks * width / (seqs * groups))
    clip = radius / jnp.sqrt(sq_norm + 1e-06)
    clips = [clip] + [along_inner(clip, k) for k in range(1, inner)]

    whole, *clips = lax.optimization_barrier((whole, *clips))
    masked = [masked_by(whole[k], keeps[k]) for k in range(inner)]
    tokens = seqs * seq_len

    def grad_w(m, lo, hi, hid_parts):
        total = None
        for k in range(inner):
            part = masked[k][:, :, m * share:(m + 1) * share]
            scaled = (part.astype(F32) * clips[k][:, None, None]).astype(BF16)
            term = lax.dot_general(
                hid_parts[k][:, :, lo:hi].reshape(tokens, hi - lo),
                scaled.reshape(tokens, share),
                (((0,), (0,)), ((), ())),
                preferred_element_type=F32,
            )
            total = term if total is None else total + term
        return total

    def grad_h(source, lo, hi):
        total = None
        for m in range(outer):
            term = lax.dot_general(
                source[:, :, m * share:(m + 1) * share].reshape(tokens, share),
                w_parts[m][lo:hi],
                (((1,), (1,)), ((), ())),
                preferred_element_type=F32,
            )
            total = term if total is None else total + term
        return total

    cuts = pieces(units, 3)
    w_first = [grad_w(m, *cuts[0], hid_parts).astype(BF16) for m in range(1, outer)]
    others, w_first = lax.optimization_barrier((masked[1:], w_first))
    h_terms = []
    for cut in cuts:
        terms = [grad_h(value, *cut).astype(BF16) for value in others]
        others, terms = lax.optimization_barrier((others, terms))
        h_terms.append(terms)
    w_terms = [w_first] + [
        [grad_w(m, *cut, hid_parts).astype(BF16) for m in range(1, outer)] for cut in cuts[1:]
    ]
    grad_w_in = [[along_outer(terms[m - 1], -m) for m in range(1, outer)] for terms in w_terms]
    grad_h_in = [[along_inner(terms[k - 1], -k) for k in range(1, inner)] for terms in h_terms]

    own_w, own_h = lax.optimization_barrier((grad_w(0, 0, units, hid_parts), grad_h(masked[0], 0, units)))
    own_w = with_layout_constraint(own_w, Layout(major_to_minor=(0, 1)))
    for k in range(inner - 1):
        own_h = own_h + jnp.concatenate([parts[k] for parts in grad_h_in], axis=1).astype(F32)
    for m in range(outer - 1):
        own_w = own_w + jnp.concatenate([parts[m] for parts in grad_w_in], axis=0).astype(F32)
    return (own_w, own_h.astype(BF16).reshape(seqs, seq_len, units))


def solution(mesh):
    in_specs = (P("dp", None, "mp"), P("dp", "mp", None), P("mp", "dp"), P("dp"))
    out_specs = (P("mp", "dp"), P("dp", None, "mp"))
    return jax.shard_map(body, mesh=mesh, in_specs=in_specs, out_specs=out_specs, check_vma=False)
```
